32 devices in a mesh: space: 4 (over z), member: 4 (over y, x), lag: 2 (over core).
Axes of the slice: x: 2, y: 2, z: 4, core: 2. Of those that a mesh axis runs over, the one named last changes fastest.
Arguments:
- anomalies: bfloat16 [2, 16384, 512], P('lag', 'space', 'member'), may hold values from -6 to 6
- mean_state: float32 [2, 16384], P('lag', 'space'), may hold values from -6 to 6
- footprints: bfloat16 [4, 2, 16, 256, 512], P(None, 'lag', 'space'), may hold values from -0.09375 to 0.09375
- slot_tiles: int32 [4, 2, 16], P(None, 'lag', 'space'), may hold values from 0 to 7, as said below
- slot_counts: int32 [4, 2, 4], P(None, 'lag', 'space'), may hold values from 0 to 4, as said below
- obs_values: float32 [4, 4, 256], P('space'), may hold values from -6 to 6
- obs_errors: float32 [4, 4, 256], P('space'), may hold values from 0.5 to 1.5
- owners: int32 [4], replicated, may hold values from 0 to 3
- batch_order: int32 [4], replicated, may hold values from 0 to 3, as said below
Outputs:
- analysis_anoms: bfloat16 [2, 16384, 512], P('lag', 'space', 'member')
- analysis_mean: float32 [2, 16384], P('lag', 'space')
The draws below stay inside these ranges and needn't reach their ends.
Inputs may be any that keep to these rules, and one draw needn't show every extreme that they name: `slot_counts`: in every batch some lag week and space group has exactly 4 live slots. `slot_tiles`: within one batch, lag week and space group the 4 slots name distinct local tiles. `batch_order`: A permutation.
All inputs are finite; a program needn't handle non-finite values.
Results may differ from the reference program's by a relative error of at most 0.008.
Values may be sent and summed in bfloat16 or wider, within the bound.
A program may use at most 64 MiB of HBM per device.

```python
import math
import jax
import jax.numpy as jnp
from jax import lax

M = 512
P_SIZE = 256
TILE = 512
SLOT_DEV = 4
NB = 4
TILE_DEV = 8
LAGS = 2
CELLS = 16384
SLOTS = 16
N_SPACE = 4


def draw_slot_counts(key, part):
    key_one, key_two, key_three = jax.random.split(key, 3)
    first = jax.random.randint(key_one, (NB, LAGS, N_SPACE), 0, SLOT_DEV + 1)
    second = jax.random.randint(key_two, (NB, LAGS, N_SPACE), 0, SLOT_DEV + 1)
    counts = jnp.minimum(first, second)
    chosen = jax.random.randint(key_three, (NB, 1, 1), 0, LAGS * N_SPACE)
    position = jnp.arange(LAGS * N_SPACE).reshape(1, LAGS, N_SPACE)
    return jnp.where(position == chosen, SLOT_DEV, counts).astype(jnp.int32)


def draw_slot_tiles(key, part):
    scores = jax.random.randint(key, (NB, LAGS, N_SPACE, TILE_DEV), 0, 2 ** 20) * TILE_DEV + jnp.arange(TILE_DEV)
    ranked = jnp.argsort(scores, axis=-1, stable=True)[..., :SLOT_DEV]
    return ranked.reshape(NB, LAGS, N_SPACE * SLOT_DEV).astype(jnp.int32)


def draw_batch_order(key, part):
    order_key = jax.random.fold_in(key, 7919)
    scores = jax.random.randint(order_key, (NB,), 0, 2 ** 20) * NB + jnp.arange(NB)
    return jnp.argsort(scores, stable=True).astype(jnp.int32)


def with_ends(drawn, stream_key, smallest, top_value):
    index_at = [jax.random.randint(jax.random.fold_in(stream_key, axis), (), 0, length) for axis, length in enumerate(drawn.shape)]
    main_axis = drawn.shape.index(max(drawn.shape))
    next_to = index_at[:main_axis] + [(index_at[main_axis] + 1) % drawn.shape[main_axis]] + index_at[main_axis + 1:]
    return drawn.at[tuple(index_at)].set(smallest).at[tuple(next_to)].set(top_value)


def shard_levels(rng, extent, shards, least, largest):
    gain, own = 1.0, jax.random.fold_in(rng, 6)
    for dim, blocks in shards:
        draws = jnp.exp(jax.random.uniform(jax.random.fold_in(own, dim), (blocks,), jnp.float32, least / len(shards), largest / len(shards)))
        gain = gain * jnp.repeat(draws, extent[dim] // blocks).reshape([-1 if axis == dim else 1 for axis in range(len(extent))])
    return gain


def bell_draw(own_key, dims, spread, most, pieces=(), kind=jnp.bfloat16):
    gain = shard_levels(own_key, dims, pieces, -0.22, 0.18) if pieces else 1.0
    entries = jax.random.normal(own_key, dims, jnp.float32) * spread * gain
    return jnp.minimum(jnp.maximum(entries, -most), most).astype(kind)


def setup_inputs(seed: int = 0) -> dict:
    splits = jax.random.split(jax.random.key(seed), 10)
    anomalies = bell_draw(splits[0], (LAGS, CELLS, M), 1.0, 6.0, ((0, 2), (1, 4), (2, 4)))
    mean_state = bell_draw(splits[1], (LAGS, CELLS), 1.0, 6.0, ((0, 2), (1, 4)), jnp.float32)
    footprints = bell_draw(splits[2], (NB, LAGS, SLOTS, P_SIZE, TILE), (TILE * SLOTS * LAGS // 4) ** -0.5, 0.09375, ((1, 2), (2, 4)))
    slot_tiles = draw_slot_tiles(jax.random.fold_in(splits[9], 71), 0)
    slot_counts = draw_slot_counts(jax.random.fold_in(splits[9], 71), 0)
    obs_values = bell_draw(splits[5], (N_SPACE, NB, P_SIZE), 1.0, 6.0, ((0, 4),), jnp.float32)
    obs_errors = jnp.clip(jnp.exp(math.log(1.5) - 1.0986123 * jax.random.uniform(splits[6], (N_SPACE, NB, P_SIZE), jnp.float32) ** shard_levels(splits[6], (N_SPACE, NB, P_SIZE), ((0, 4),), -0.2, 0.2)), 0.5, 1.5)
    owners = with_ends(jax.random.randint(splits[7], (NB,), 0, N_SPACE), jax.random.fold_in(splits[7], 1), 0, N_SPACE - 1).astype(jnp.int32)
    batch_order = draw_batch_order(jax.random.fold_in(splits[9], 71), 0)
    return {"anomalies": anomalies, "mean_state": mean_state, "footprints": footprints, "slot_tiles": slot_tiles, "slot_counts": slot_counts, "obs_values": obs_values, "obs_errors": obs_errors, "owners": owners, "batch_order": batch_order}


def innovation(obs_round, values_now, obs_means, errors_now, members):
    obs_total = obs_round.shape[0]
    innov_cov = jnp.dot(obs_round.astype(jnp.float32), obs_round.T.astype(jnp.float32), preferred_element_type=jnp.float32) / (members - 1) + jnp.diag(errors_now * errors_now)
    factor = jnp.linalg.cholesky(innov_cov)
    identity = jnp.eye(obs_total, dtype=jnp.float32)
    inverse_sum = lax.linalg.triangular_solve(factor + jnp.diag(errors_now), identity, left_side=True, lower=True)
    transform = lax.linalg.triangular_solve(factor, inverse_sum, left_side=True, lower=True, transpose_a=True)
    forward = lax.linalg.triangular_solve(factor, (values_now - obs_means)[:, None], left_side=True, lower=True)
    weights_obs = lax.linalg.triangular_solve(factor, forward, left_side=True, lower=True, transpose_a=True)[:, 0]
    return (transform, weights_obs)

def reference(anomalies, mean_state, footprints, slot_tiles, slot_counts, obs_values, obs_errors, owners, batch_order):
    highest = lax.Precision.HIGHEST
    tile_total = N_SPACE * TILE_DEV
    tile_anoms = anomalies.reshape(LAGS, tile_total, TILE, M)
    tile_means = mean_state.reshape(LAGS, tile_total, TILE)
    slot_group = (jnp.arange(SLOTS) // SLOT_DEV).astype(jnp.int32)
    slot_place = (jnp.arange(SLOTS) % SLOT_DEV).astype(jnp.int32)
    lag_ids = jnp.arange(LAGS).astype(jnp.int32)[:, None]
    for position in range(NB):
        batch_now = batch_order[position]
        values_now = obs_values[owners[batch_now], batch_now]
        errors_now = obs_errors[owners[batch_now], batch_now]
        global_ids = slot_group[None, :] * TILE_DEV + slot_tiles[batch_now]
        live_mask = slot_place[None, :] < slot_counts[batch_now][:, slot_group]
        slot_anoms = tile_anoms[lag_ids, global_ids]
        slot_means = tile_means[lag_ids, global_ids]
        prints = footprints[batch_now].astype(jnp.float32)
        masked = jnp.where(live_mask[:, :, None, None], slot_anoms, 0).astype(jnp.float32)
        obs_anoms = jnp.einsum('lspt,lstm->pm', prints, masked)
        mean_round = jnp.where(live_mask[:, :, None], slot_means.astype(jnp.bfloat16), 0).astype(jnp.float32)
        obs_means = jnp.einsum('lspt,lst->p', prints, mean_round)
        obs_round = obs_anoms.astype(jnp.bfloat16)
        transform, weights_obs = innovation(obs_round, values_now, obs_means, errors_now, M)
        wide_anoms = slot_anoms.astype(jnp.float32)
        wide_obs = obs_round.astype(jnp.float32)
        covariance = jnp.einsum('lstm,pm->lstp', wide_anoms, wide_obs)
        gain_tile = (jnp.einsum('lstp,pq->lstq', covariance, transform, precision=highest) / (M - 1)).astype(jnp.bfloat16)
        updated = (wide_anoms - jnp.einsum('lstp,pm->lstm', gain_tile.astype(jnp.float32), wide_obs)).astype(jnp.bfloat16)
        tile_anoms = tile_anoms.at[lag_ids, global_ids].set(jnp.where(live_mask[:, :, None, None], updated, slot_anoms))
        shifted = slot_means + jnp.einsum('lstp,p->lst', covariance, weights_obs, precision=highest) / (M - 1)
        tile_means = tile_means.at[lag_ids, global_ids].set(jnp.where(live_mask[:, :, None], shifted, slot_means))
    return (tile_anoms.reshape(LAGS, CELLS, M), tile_means.reshape(LAGS, CELLS))
```

```python
import functools

import jax
import jax.numpy as jnp
from jax import lax
from jax.experimental import pallas as pl
from jax.experimental.pallas import tpu as pltpu
from jax.sharding import PartitionSpec as P

HIGH = lax.Precision.HIGHEST
BF = jnp.bfloat16
F32 = jnp.float32
BLK = 64


def prints_kernel(order, tiles, dest, f_ref, x_ref, p_ref, m_ref, acc):
    step = pl.program_id(0)

    @pl.when(step == 0)
    def _():
        acc[...] = jnp.zeros_like(acc)

    part = jnp.dot(f_ref[0, 0], x_ref[0], preferred_element_type=F32)
    acc[dest[step]] += part

    @pl.when(step == pl.num_programs(0) - 1)
    def _():
        count = p_ref.shape[0]
        p_ref[...] = acc[:count, :, : p_ref.shape[2]].astype(BF)
        m_ref[...] = acc[:count, :, p_ref.shape[2] :]


def factor(block, errs):
    lanes = lax.broadcasted_iota(jnp.int32, (1, 2 * BLK), 1)
    a = block
    both_row = lax.broadcasted_iota(jnp.int32, (BLK, 2 * BLK), 0)
    both_col = lax.broadcasted_iota(jnp.int32, (BLK, 2 * BLK), 1)
    both = jnp.where(lax.rem(both_col, BLK) == both_row, 1.0, 0.0).astype(F32)
    done = []
    for group in range(BLK // 8):
        rows = BLK - 8 * group
        row_id = lax.broadcasted_iota(jnp.int32, (rows, 1), 0)
        row_wide = lax.broadcasted_iota(jnp.int32, (rows, 2 * BLK), 0)
        for i in range(8):
            k = 8 * group + i
            pivot = a[i : i + 1, k : k + 1]
            root = lax.rsqrt(pivot)
            below = jnp.where(row_id > i, a[:, k : k + 1] * root, 0.0)
            row = a[i : i + 1, :] * root
            scale = jnp.where(lanes < BLK, root, 1.0 / (pivot * root + errs[k : k + 1, :]))
            both_k = both[i : i + 1, :] * scale
            a = a - below * row
            both = jnp.where(row_wide == i, both_k, both - below * both_k)
        done.append(both[:8])
        a = a[8:]
        both = both[8:]
    full = jnp.concatenate(done, axis=0)
    return full[:, :BLK], full[:, BLK:]


def chain_kernel(
    own_ref, p_ref, m_ref, val_ref, err_ref, c_ref, ps, ms, qs, cov, inv, inv_sum
):
    batches = pl.num_programs(0)
    total = 4
    k_now = pl.program_id(0)
    groups, mats, obs, width = p_ref.shape
    members = groups * width

    @pl.when(k_now == 0)
    def _():
        for g in range(groups):
            ps[:, :, g * width : (g + 1) * width] = p_ref[g]
        ms[...] = m_ref[...]

    here = lax.shift_left(1, k_now) - 1
    y = ps[here]
    errs = err_ref[0]
    rows = lax.broadcasted_iota(jnp.int32, (obs, obs), 0)
    cols = lax.broadcasted_iota(jnp.int32, (obs, obs), 1)
    gram = lax.dot_general(y, y, (((1,), (1,)), ((), ())), preferred_element_type=F32)
    cov[...] = gram / (members - 1) + jnp.where(rows == cols, errs * errs, 0.0)
    unit = jnp.where(rows == cols, 1.0, 0.0).astype(F32)
    inv[...] = unit
    inv_sum[...] = unit
    lane = lax.broadcasted_iota(jnp.int32, (BLK, obs), 1)

    def block_step(j, carry):
        at = pl.ds(pl.multiple_of(j * BLK, BLK), BLK)
        strip = cov[at, :]
        diag = strip[:, :BLK]
        for c in range(1, obs // BLK):
            diag = jnp.where(j == c, strip[:, c * BLK : (c + 1) * BLK], diag)
        low, low_sum = factor(diag, err_ref[0, at, :])
        upper = jnp.dot(low, strip, precision=HIGH, preferred_element_type=F32)
        upper = jnp.where(lane >= (j + 1) * BLK, upper, 0.0)
        row_inv = jnp.dot(low, inv[at, :], precision=HIGH, preferred_element_type=F32)
        row_sum = jnp.dot(low_sum, inv_sum[at, :], precision=HIGH, preferred_element_type=F32)
        inv[at, :] = row_inv
        inv_sum[at, :] = row_sum
        wide = jnp.concatenate([upper, row_inv, row_sum], axis=1)
        drop = jnp.dot(upper.T, wide, precision=HIGH, preferred_element_type=F32)
        cov[...] -= drop[:, :obs]
        inv[...] -= drop[:, obs : 2 * obs]
        inv_sum[...] -= drop[:, 2 * obs :]
        return carry

    lax.fori_loop(0, obs // BLK, block_step, 0)
    lower_inv = inv[...]
    miss = ms[here] - val_ref[0]
    right = jnp.concatenate(
        [
            jnp.dot(inv_sum[...], y.astype(F32), precision=HIGH, preferred_element_type=F32),
            jnp.dot(lower_inv, miss, precision=HIGH, preferred_element_type=F32),
        ],
        axis=1,
    )
    weights = jnp.dot(lower_inv.T, right, precision=HIGH, preferred_element_type=F32)
    q = lax.dot_general(
        y, weights.astype(BF), (((0,), (0,)), ((), ())), preferred_element_type=F32
    ) / (members - 1)
    qs[k_now] = q.astype(BF)

    for k in range(total - 1):

        @pl.when(k_now == k)
        def _(k=k):
            qk = qs[k]
            for b in range(k + 1, total):
                base = 2**b - 1
                for s in range(0, 2**b, 2 ** (k + 1)):
                    keep, move = base + s, base + s + 2**k
                    source = ps[move]
                    change = jnp.dot(source, qk, preferred_element_type=F32)
                    ps[keep] = (
                        ps[keep].astype(F32) + source.astype(F32) - change[:, :members]
                    ).astype(BF)
                    ms[keep] = ms[keep] + ms[move] - change[:, members:]

    @pl.when(k_now == batches - 1)
    def _():
        c_ref[0] = jnp.zeros(c_ref.shape[1:], BF)
        own = pl.ds(pl.multiple_of(own_ref[0] * width, width), width)
        for k in range(total - 1, -1, -1):
            term = jnp.concatenate([qs[k, :, own], qs[k, :, members:]], axis=1)
            c_ref[2**k] = term
            for s in range(2 ** (k + 1), 2**total, 2 ** (k + 1)):
                prior = c_ref[s]
                c_ref[s + 2**k] = (
                    prior.astype(F32)
                    + term.astype(F32)
                    - jnp.dot(qs[k, :, :members], prior, preferred_element_type=F32)
                ).astype(BF)


def final_kernel(history, x_ref, all_ref, mean_ref, c_ref, out_ref, mean_out):
    groups, _, width = all_ref.shape
    change = jnp.zeros((x_ref.shape[1], 2 * width), F32)
    for g in range(groups):
        change += jnp.dot(
            all_ref[g], c_ref[0, g * width : (g + 1) * width, :], preferred_element_type=F32
        )
    out_ref[0] = (x_ref[0].astype(F32) - change[:, :width]).astype(BF)
    shift = change[:, width:].T[0:1, :]
    mean_out[0] = mean_ref[0] - shift


def body(
    anomalies,
    mean_state,
    footprints,
    slot_tiles,
    slot_counts,
    obs_values,
    obs_errors,
    owners,
    batch_order,
):
    batches, _, slot_dev, obs, tile_cells = footprints.shape
    width = anomalies.shape[2]
    groups = lax.axis_size("member")
    members = width * groups
    tiles = anomalies.shape[1] // tile_cells
    mats = 2**batches - 1
    x = anomalies[0].reshape(tiles, tile_cells, width)
    means = mean_state[0].reshape(tiles, 1, tile_cells)
    x_all = lax.all_gather(anomalies[0], "member", axis=0)

    ids = slot_tiles[:, 0][batch_order]
    counts = slot_counts[:, 0, 0][batch_order]
    live = jnp.arange(slot_dev)[None, :] < counts[:, None]
    tile_live = jnp.any(
        (ids[:, :, None] == jnp.arange(tiles)) & live[:, :, None], axis=1
    ).astype(jnp.int32)
    bits = jnp.left_shift(1, jnp.arange(batches))[:, None] * tile_live
    history = jnp.sum(bits, axis=0)
    before = jnp.cumsum(bits, axis=0) - bits
    slot_before = jnp.take_along_axis(before, ids, axis=1)
    base = (jnp.left_shift(1, jnp.arange(batches)) - 1)[:, None]
    dest = jnp.where(live, base + slot_before, mats).astype(jnp.int32).reshape(-1)

    mean_pad = jnp.pad(
        mean_state[0].astype(BF).reshape(tiles, tile_cells, 1), ((0, 0), (0, 0), (0, width - 1))
    )
    x_mean = jnp.concatenate([x, mean_pad], axis=2)
    part, part_mean = pl.pallas_call(
        prints_kernel,
        out_shape=(
            jax.ShapeDtypeStruct((mats, obs, width), BF),
            jax.ShapeDtypeStruct((mats, obs, width), F32),
        ),
        grid_spec=pltpu.PrefetchScalarGridSpec(
            num_scalar_prefetch=3,
            grid=(batches * slot_dev,),
            in_specs=[
                pl.BlockSpec(
                    (1, 1, obs, tile_cells),
                    lambda i, o, t, d: (o[i // slot_dev], i % slot_dev, 0, 0),
                ),
                pl.BlockSpec((1, tile_cells, 2 * width), lambda i, o, t, d: (t[i], 0, 0)),
            ],
            out_specs=[
                pl.BlockSpec((mats, obs, width), lambda i, o, t, d: (0, 0, 0)),
                pl.BlockSpec((mats, obs, width), lambda i, o, t, d: (0, 0, 0)),
            ],
            scratch_shapes=[pltpu.VMEM((mats + 1, obs, 2 * width), F32)],
        ),
        compiler_params=pltpu.CompilerParams(vmem_limit_bytes=40 * 2**20),
        name="prints",
    )(batch_order, ids.reshape(-1), dest, footprints[:, 0], x_mean)

    small = jnp.concatenate(
        [part_mean[:, :, 0], obs_values[0], obs_errors[0]], axis=0
    )
    small_all = lax.all_gather(small, ("space", "lag"), axis=0)
    mean_sum = jnp.sum(small_all[:, :mats], axis=0)
    lags = lax.axis_size("lag")
    owner_row = owners[batch_order] * lags
    values = small_all[owner_row, mats + batch_order]
    errors = small_all[owner_row, mats + batches + batch_order]

    summed = lax.psum(part, ("space", "lag"))
    p_all = lax.all_gather(summed, "member", axis=0)
    own = lax.axis_index("member").astype(jnp.int32).reshape(1)
    mean_cols = jnp.pad(mean_sum[:, :, None], ((0, 0), (0, 0), (0, width - 1)))

    states = pl.pallas_call(
        chain_kernel,
        out_shape=jax.ShapeDtypeStruct((2**batches, members, 2 * width), BF),
        grid_spec=pltpu.PrefetchScalarGridSpec(
            num_scalar_prefetch=1,
            grid=(batches,),
            in_specs=[
                pl.BlockSpec((groups, mats, obs, width), lambda k, o: (0, 0, 0, 0)),
                pl.BlockSpec((mats, obs, width), lambda k, o: (0, 0, 0)),
                pl.BlockSpec((1, obs, 1), lambda k, o: (k, 0, 0)),
                pl.BlockSpec((1, obs, 1), lambda k, o: (k, 0, 0)),
            ],
            out_specs=pl.BlockSpec(
                (2**batches, members, 2 * width), lambda k, o: (0, 0, 0)
            ),
            scratch_shapes=[
                pltpu.VMEM((mats, obs, members), BF),
                pltpu.VMEM((mats, obs, width), F32),
                pltpu.VMEM((batches, members, members + width), BF),
                pltpu.VMEM((obs, obs), F32),
                pltpu.VMEM((obs, obs), F32),
                pltpu.VMEM((obs, obs), F32),
            ],
        ),
        compiler_params=pltpu.CompilerParams(vmem_limit_bytes=56 * 2**20),
        cost_estimate=pl.CostEstimate(
            flops=20 * 10**9, bytes_accessed=10**7, transcendentals=0
        ),
        name="chain",
    )(own, p_all, mean_cols, values[:, :, None], errors[:, :, None])

    new_x, new_mean = pl.pallas_call(
        final_kernel,
        out_shape=(
            jax.ShapeDtypeStruct((tiles, tile_cells, width), BF),
            jax.ShapeDtypeStruct((tiles, 1, tile_cells), F32),
        ),
        grid_spec=pltpu.PrefetchScalarGridSpec(
            num_scalar_prefetch=1,
            grid=(tiles,),
            in_specs=[
                pl.BlockSpec((1, tile_cells, width), lambda t, h: (t, 0, 0)),
                pl.BlockSpec((groups, tile_cells, width), lambda t, h: (0, t, 0)),
                pl.BlockSpec((1, 1, tile_cells), lambda t, h: (t, 0, 0)),
                pl.BlockSpec((1, members, 2 * width), lambda t, h: (h[t], 0, 0)),
            ],
            out_specs=[
                pl.BlockSpec((1, tile_cells, width), lambda t, h: (t, 0, 0)),
                pl.BlockSpec((1, 1, tile_cells), lambda t, h: (t, 0, 0)),
            ],
        ),
        name="final",
    )(history, x, x_all, means, states)
    return (new_x.reshape(1, -1, width), new_mean.reshape(1, -1))


def solution(mesh):
    return jax.shard_map(
        body,
        mesh=mesh,
        in_specs=(
            P("lag", "space", "member"),
            P("lag", "space"),
            P(None, "lag", "space", None, None),
            P(None, "lag", "space"),
            P(None, "lag", "space"),
            P("space", None, None),
            P("space", None, None),
            P(),
            P(),
        ),
        out_specs=(P("lag", "space", "member"), P("lag", "space")),
        check_vma=False,
    )
```

```python
import functools

import jax
import jax.numpy as jnp
from jax import lax
from jax.experimental import pallas as pl
from jax.experimental.pallas import tpu as pltpu
from jax.sharding import PartitionSpec as P

HIGH = lax.Precision.HIGHEST
BF = jnp.bfloat16
F32 = jnp.float32
BLK = 64


def prints_kernel(order, tiles, dest, f_ref, x_ref, p_ref, m_ref, acc):
    step = pl.program_id(0)

    @pl.when(step == 0)
    def _():
        acc[...] = jnp.zeros_like(acc)

    part = jnp.dot(f_ref[0, 0], x_ref[0], preferred_element_type=F32)
    acc[dest[step]] += part

    @pl.when(step == pl.num_programs(0) - 1)
    def _():
        count = p_ref.shape[0]
        p_ref[...] = acc[:count, :, : p_ref.shape[2]].astype(BF)
        m_ref[...] = acc[:count, :, p_ref.shape[2] :]


def factor(block, errs):
    lanes = lax.broadcasted_iota(jnp.int32, (1, 2 * BLK), 1)
    a = block
    both_row = lax.broadcasted_iota(jnp.int32, (BLK, 2 * BLK), 0)
    both_col = lax.broadcasted_iota(jnp.int32, (BLK, 2 * BLK), 1)
    both = jnp.where(lax.rem(both_col, BLK) == both_row, 1.0, 0.0).astype(F32)
    done = []
    for group in range(BLK // 8):
        rows = BLK - 8 * group
        row_wide = lax.broadcasted_iota(jnp.int32, (rows, 2 * BLK), 0)
        for start in range(0, 8, 4):
            lead = [
                jnp.broadcast_to(a[:, k : k + 1], (rows, 2 * BLK))
                for k in range(8 * group + start, 8 * group + start + 4)
            ]
            for m in range(4):
                i = start + m
                k = 8 * group + i
                pivot = lead[m][i : i + 1, :]
                root = lax.rsqrt(pivot)
                below = jnp.where(row_wide > i, lead[m] * root, 0.0)
                for n in range(m + 1, 4):
                    lead[n] = lead[n] - below * below[start + n : start + n + 1, :]
                row = a[i : i + 1, :] * root[:, :BLK]
                scale = jnp.where(lanes < BLK, root, 1.0 / (pivot * root + errs[k : k + 1, :]))
                both_k = both[i : i + 1, :] * scale
                a = a - below[:, :BLK] * row
                both = jnp.where(row_wide == i, both_k, both - below * both_k)
        done.append(both[:8])
        a = a[8:]
        both = both[8:]
    full = jnp.concatenate(done, axis=0)
    return full[:, :BLK], full[:, BLK:]


def chain_kernel(
    own_ref, p_ref, m_ref, val_ref, err_ref, c_ref, ps, ms, qs, cov, inv, inv_sum
):
    batches = pl.num_programs(0)
    total = 4
    k_now = pl.program_id(0)
    groups, mats, obs, width = p_ref.shape
    members = groups * width

    @pl.when(k_now == 0)
    def _():
        for g in range(groups):
            ps[:, :, g * width : (g + 1) * width] = p_ref[g]
        ms[...] = m_ref[...]

    here = lax.shift_left(1, k_now) - 1
    y = ps[here]
    errs = err_ref[0]
    rows = lax.broadcasted_iota(jnp.int32, (obs, obs), 0)
    cols = lax.broadcasted_iota(jnp.int32, (obs, obs), 1)
    gram = lax.dot_general(y, y, (((1,), (1,)), ((), ())), preferred_element_type=F32)
    cov[...] = gram / (members - 1) + jnp.where(rows == cols, errs * errs, 0.0)
    unit = jnp.where(rows == cols, 1.0, 0.0).astype(F32)
    inv[...] = unit
    inv_sum[...] = unit
    lane = lax.broadcasted_iota(jnp.int32, (BLK, obs), 1)

    def block_step(j, carry):
        at = pl.ds(pl.multiple_of(j * BLK, BLK), BLK)
        strip = cov[at, :]
        diag = strip[:, :BLK]
        for c in range(1, obs // BLK):
            diag = jnp.where(j == c, strip[:, c * BLK : (c + 1) * BLK], diag)
        low, low_sum = factor(diag, err_ref[0, at, :])
        upper = jnp.dot(low, strip, precision=HIGH, preferred_element_type=F32)
        upper = jnp.where(lane >= (j + 1) * BLK, upper, 0.0)
        row_inv = jnp.dot(low, inv[at, :], precision=HIGH, preferred_element_type=F32)
        row_sum = jnp.dot(low_sum, inv_sum[at, :], precision=HIGH, preferred_element_type=F32)
        inv[at, :] = row_inv
        inv_sum[at, :] = row_sum
        wide = jnp.concatenate([upper, row_inv, row_sum], axis=1)
        drop = jnp.dot(upper.T, wide, precision=HIGH, preferred_element_type=F32)
        cov[...] -= drop[:, :obs]
        inv[...] -= drop[:, obs : 2 * obs]
        inv_sum[...] -= drop[:, 2 * obs :]
        return carry

    lax.fori_loop(0, obs // BLK, block_step, 0)
    lower_inv = inv[...]
    miss = ms[here] - val_ref[0]
    right = jnp.concatenate(
        [
            jnp.dot(inv_sum[...], y.astype(F32), precision=HIGH, preferred_element_type=F32),
            jnp.dot(lower_inv, miss, precision=HIGH, preferred_element_type=F32),
        ],
        axis=1,
    )
    weights = jnp.dot(lower_inv.T, right, precision=HIGH, preferred_element_type=F32)
    q = lax.dot_general(
        y, weights.astype(BF), (((0,), (0,)), ((), ())), preferred_element_type=F32
    ) / (members - 1)
    qs[k_now] = q.astype(BF)

    for k in range(total - 1):

        @pl.when(k_now == k)
        def _(k=k):
            qk = qs[k]
            for b in range(k + 1, total):
                base = 2**b - 1
                for s in range(0, 2**b, 2 ** (k + 1)):
                    keep, move = base + s, base + s + 2**k
                    source = ps[move]
                    change = jnp.dot(source, qk, preferred_element_type=F32)
                    ps[keep] = (
                        ps[keep].astype(F32) + source.astype(F32) - change[:, :members]
                    ).astype(BF)
                    ms[keep] = ms[keep] + ms[move] - change[:, members:]

    @pl.when(k_now == batches - 1)
    def _():
        c_ref[0] = jnp.zeros(c_ref.shape[1:], BF)
        own = pl.ds(pl.multiple_of(own_ref[0] * width, width), width)
        for k in range(total - 1, -1, -1):
            term = jnp.concatenate([qs[k, :, own], qs[k, :, members:]], axis=1)
            c_ref[2**k] = term
            for s in range(2 ** (k + 1), 2**total, 2 ** (k + 1)):
                prior = c_ref[s]
                c_ref[s + 2**k] = (
                    prior.astype(F32)
                    + term.astype(F32)
                    - jnp.dot(qs[k, :, :members], prior, preferred_element_type=F32)
                ).astype(BF)


def final_kernel(history, x_ref, all_ref, mean_ref, c_ref, out_ref, mean_out):
    groups, _, width = all_ref.shape
    change = jnp.zeros((x_ref.shape[1], 2 * width), F32)
    for g in range(groups):
        change += jnp.dot(
            all_ref[g], c_ref[0, g * width : (g + 1) * width, :], preferred_element_type=F32
        )
    out_ref[0] = (x_ref[0].astype(F32) - change[:, :width]).astype(BF)
    shift = change[:, width:].T[0:1, :]
    mean_out[0] = mean_ref[0] - shift


def body(
    anomalies,
    mean_state,
    footprints,
    slot_tiles,
    slot_counts,
    obs_values,
    obs_errors,
    owners,
    batch_order,
):
    batches, _, slot_dev, obs, tile_cells = footprints.shape
    width = anomalies.shape[2]
    groups = lax.axis_size("member")
    members = width * groups
    tiles = anomalies.shape[1] // tile_cells
    mats = 2**batches - 1
    x = anomalies[0].reshape(tiles, tile_cells, width)
    means = mean_state[0].reshape(tiles, 1, tile_cells)
    x_all = lax.all_gather(anomalies[0], "member", axis=0)

    ids = slot_tiles[:, 0][batch_order]
    counts = slot_counts[:, 0, 0][batch_order]
    live = jnp.arange(slot_dev)[None, :] < counts[:, None]
    tile_live = jnp.any(
        (ids[:, :, None] == jnp.arange(tiles)) & live[:, :, None], axis=1
    ).astype(jnp.int32)
    bits = jnp.left_shift(1, jnp.arange(batches))[:, None] * tile_live
    history = jnp.sum(bits, axis=0)
    before = jnp.cumsum(bits, axis=0) - bits
    slot_before = jnp.take_along_axis(before, ids, axis=1)
    base = (jnp.left_shift(1, jnp.arange(batches)) - 1)[:, None]
    dest = jnp.where(live, base + slot_before, mats).astype(jnp.int32).reshape(-1)

    mean_pad = jnp.pad(
        mean_state[0].astype(BF).reshape(tiles, tile_cells, 1), ((0, 0), (0, 0), (0, width - 1))
    )
    x_mean = jnp.concatenate([x, mean_pad], axis=2)
    part, part_mean = pl.pallas_call(
        prints_kernel,
        out_shape=(
            jax.ShapeDtypeStruct((mats, obs, width), BF),
            jax.ShapeDtypeStruct((mats, obs, width), F32),
        ),
        grid_spec=pltpu.PrefetchScalarGridSpec(
            num_scalar_prefetch=3,
            grid=(batches * slot_dev,),
            in_specs=[
                pl.BlockSpec(
                    (1, 1, obs, tile_cells),
                    lambda i, o, t, d: (o[i // slot_dev], i % slot_dev, 0, 0),
                ),
                pl.BlockSpec((1, tile_cells, 2 * width), lambda i, o, t, d: (t[i], 0, 0)),
            ],
            out_specs=[
                pl.BlockSpec((mats, obs, width), lambda i, o, t, d: (0, 0, 0)),
                pl.BlockSpec((mats, obs, width), lambda i, o, t, d: (0, 0, 0)),
            ],
            scratch_shapes=[pltpu.VMEM((mats + 1, obs, 2 * width), F32)],
        ),
        compiler_params=pltpu.CompilerParams(vmem_limit_bytes=40 * 2**20),
        name="prints",
    )(batch_order, ids.reshape(-1), dest, footprints[:, 0], x_mean)

    small = jnp.concatenate(
        [part_mean[:, :, 0], obs_values[0], obs_errors[0]], axis=0
    )
    small_all = lax.all_gather(small, ("space", "lag"), axis=0)
    mean_sum = jnp.sum(small_all[:, :mats], axis=0)
    lags = lax.axis_size("lag")
    owner_row = owners[batch_order] * lags
    values = small_all[owner_row, mats + batch_order]
    errors = small_all[owner_row, mats + batches + batch_order]

    summed = lax.psum_scatter(
        part.reshape(mats * obs, width), ("space", "lag"), scatter_dimension=0, tiled=True
    )
    summed, values, errors, mean_sum = lax.optimization_barrier(
        (summed, values, errors, mean_sum)
    )
    p_all = lax.all_gather(summed, ("member", "space", "lag"), axis=0, tiled=True)
    p_all = p_all.reshape(groups, mats, obs, width)
    own = lax.axis_index("member").astype(jnp.int32).reshape(1)
    mean_cols = jnp.pad(mean_sum[:, :, None], ((0, 0), (0, 0), (0, width - 1)))

    states = pl.pallas_call(
        chain_kernel,
        out_shape=jax.ShapeDtypeStruct((2**batches, members, 2 * width), BF),
        grid_spec=pltpu.PrefetchScalarGridSpec(
            num_scalar_prefetch=1,
            grid=(batches,),
            in_specs=[
                pl.BlockSpec((groups, mats, obs, width), lambda k, o: (0, 0, 0, 0)),
                pl.BlockSpec((mats, obs, width), lambda k, o: (0, 0, 0)),
                pl.BlockSpec((1, obs, 1), lambda k, o: (k, 0, 0)),
                pl.BlockSpec((1, obs, 1), lambda k, o: (k, 0, 0)),
            ],
            out_specs=pl.BlockSpec(
                (2**batches, members, 2 * width), lambda k, o: (0, 0, 0)
            ),
            scratch_shapes=[
                pltpu.VMEM((mats, obs, members), BF),
                pltpu.VMEM((mats, obs, width), F32),
                pltpu.VMEM((batches, members, members + width), BF),
                pltpu.VMEM((obs, obs), F32),
                pltpu.VMEM((obs, obs), F32),
                pltpu.VMEM((obs, obs), F32),
            ],
        ),
        compiler_params=pltpu.CompilerParams(vmem_limit_bytes=56 * 2**20),
        cost_estimate=pl.CostEstimate(
            flops=20 * 10**9, bytes_accessed=10**7, transcendentals=0
        ),
        name="chain",
    )(own, p_all, mean_cols, values[:, :, None], errors[:, :, None])

    new_x, new_mean = pl.pallas_call(
        final_kernel,
        out_shape=(
            jax.ShapeDtypeStruct((tiles, tile_cells, width), BF),
            jax.ShapeDtypeStruct((tiles, 1, tile_cells), F32),
        ),
        grid_spec=pltpu.PrefetchScalarGridSpec(
            num_scalar_prefetch=1,
            grid=(tiles,),
            in_specs=[
                pl.BlockSpec((1, tile_cells, width), lambda t, h: (t, 0, 0)),
                pl.BlockSpec((groups, tile_cells, width), lambda t, h: (0, t, 0)),
                pl.BlockSpec((1, 1, tile_cells), lambda t, h: (t, 0, 0)),
                pl.BlockSpec((1, members, 2 * width), lambda t, h: (h[t], 0, 0)),
            ],
            out_specs=[
                pl.BlockSpec((1, tile_cells, width), lambda t, h: (t, 0, 0)),
                pl.BlockSpec((1, 1, tile_cells), lambda t, h: (t, 0, 0)),
            ],
        ),
        name="final",
    )(history, x, x_all, means, states)
    return (new_x.reshape(1, -1, width), new_mean.reshape(1, -1))


def solution(mesh):
    return jax.shard_map(
        body,
        mesh=mesh,
        in_specs=(
            P("lag", "space", "member"),
            P("lag", "space"),
            P(None, "lag", "space", None, None),
            P(None, "lag", "space"),
            P(None, "lag", "space"),
            P("space", None, None),
            P("space", None, None),
            P(),
            P(),
        ),
        out_specs=(P("lag", "space", "member"), P("lag", "space")),
        check_vma=False,
    )
```

```python
import functools

import jax
import jax.numpy as jnp
from jax import lax
from jax.experimental import pallas as pl
from jax.experimental.pallas import tpu as pltpu
from jax.sharding import PartitionSpec as P

HIGH = lax.Precision.HIGHEST
BF = jnp.bfloat16
F32 = jnp.float32
BLK = 64


def prints_kernel(order, tiles, dest, f_ref, x_ref, p_ref, m_ref, acc):
    step = pl.program_id(0)

    @pl.when(step == 0)
    def _():
        acc[...] = jnp.zeros_like(acc)

    part = jnp.dot(f_ref[0, 0], x_ref[0], preferred_element_type=F32)
    acc[dest[step]] += part

    @pl.when(step == pl.num_programs(0) - 1)
    def _():
        count = p_ref.shape[0]
        p_ref[...] = acc[:count, :, : p_ref.shape[2]].astype(BF)
        m_ref[...] = acc[:count, :, p_ref.shape[2] :]


def factor(block, errs):
    lanes = lax.broadcasted_iota(jnp.int32, (1, 2 * BLK), 1)
    a = block
    both_row = lax.broadcasted_iota(jnp.int32, (BLK, 2 * BLK), 0)
    both_col = lax.broadcasted_iota(jnp.int32, (BLK, 2 * BLK), 1)
    both = jnp.where(lax.rem(both_col, BLK) == both_row, 1.0, 0.0).astype(F32)
    done = []
    for group in range(BLK // 8):
        rows = BLK - 8 * group
        row_wide = lax.broadcasted_iota(jnp.int32, (rows, 2 * BLK), 0)
        for start in range(0, 8, 4):
            lead = [
                jnp.broadcast_to(a[:, k : k + 1], (rows, 2 * BLK))
                for k in range(8 * group + start, 8 * group + start + 4)
            ]
            for m in range(4):
                i = start + m
                k = 8 * group + i
                pivot = lead[m][i : i + 1, :]
                root = lax.rsqrt(pivot)
                below = jnp.where(row_wide > i, lead[m] * root, 0.0)
                for n in range(m + 1, 4):
                    lead[n] = lead[n] - below * below[start + n : start + n + 1, :]
                row = a[i : i + 1, :] * root[:, :BLK]
                scale = jnp.where(lanes < BLK, root, 1.0 / (pivot * root + errs[k : k + 1, :]))
                both_k = both[i : i + 1, :] * scale
                a = a - below[:, :BLK] * row
                both = jnp.where(row_wide == i, both_k, both - below * both_k)
        done.append(both[:8])
        a = a[8:]
        both = both[8:]
    full = jnp.concatenate(done, axis=0)
    return full[:, :BLK], full[:, BLK:]


def chain_kernel(
    own_ref, p_ref, m_ref, val_ref, err_ref, c_ref, ps, ms, qs, cov, inv, inv_sum
):
    batches = pl.num_programs(0)
    total = 4
    k_now = pl.program_id(0)
    lags, groups, mats, rows_in, width = p_ref.shape
    obs = lags * rows_in
    members = groups * width

    @pl.when(k_now == 0)
    def _():
        for piece in range(lags * mats):
            mat, part = divmod(piece, lags)
            for g in range(groups):
                ps[mat, part * rows_in : (part + 1) * rows_in, g * width : (g + 1) * width] = (
                    p_ref[piece // mats, g, piece % mats]
                )
        ms[...] = m_ref[...]

    here = lax.shift_left(1, k_now) - 1
    y = ps[here]
    errs = err_ref[0]
    rows = lax.broadcasted_iota(jnp.int32, (obs, obs), 0)
    cols = lax.broadcasted_iota(jnp.int32, (obs, obs), 1)
    gram = lax.dot_general(y, y, (((1,), (1,)), ((), ())), preferred_element_type=F32)
    cov[...] = gram / (members - 1) + jnp.where(rows == cols, errs * errs, 0.0)
    unit = jnp.where(rows == cols, 1.0, 0.0).astype(F32)
    inv[...] = unit
    inv_sum[...] = unit
    lane = lax.broadcasted_iota(jnp.int32, (BLK, obs), 1)

    def block_step(j, carry):
        at = pl.ds(pl.multiple_of(j * BLK, BLK), BLK)
        strip = cov[at, :]
        diag = strip[:, :BLK]
        for c in range(1, obs // BLK):
            diag = jnp.where(j == c, strip[:, c * BLK : (c + 1) * BLK], diag)
        low, low_sum = factor(diag, err_ref[0, at, :])
        upper = jnp.dot(low, strip, precision=HIGH, preferred_element_type=F32)
        upper = jnp.where(lane >= (j + 1) * BLK, upper, 0.0)
        row_inv = jnp.dot(low, inv[at, :], precision=HIGH, preferred_element_type=F32)
        row_sum = jnp.dot(low_sum, inv_sum[at, :], precision=HIGH, preferred_element_type=F32)
        inv[at, :] = row_inv
        inv_sum[at, :] = row_sum
        wide = jnp.concatenate([upper, row_inv, row_sum], axis=1)
        drop = jnp.dot(upper.T, wide, precision=HIGH, preferred_element_type=F32)
        cov[...] -= drop[:, :obs]
        inv[...] -= drop[:, obs : 2 * obs]
        inv_sum[...] -= drop[:, 2 * obs :]
        return carry

    lax.fori_loop(0, obs // BLK, block_step, 0)
    lower_inv = inv[...]
    miss = ms[here] - val_ref[0]
    right = jnp.concatenate(
        [
            jnp.dot(inv_sum[...], y.astype(F32), precision=HIGH, preferred_element_type=F32),
            jnp.dot(lower_inv, miss, precision=HIGH, preferred_element_type=F32),
        ],
        axis=1,
    )
    weights = jnp.dot(lower_inv.T, right, precision=HIGH, preferred_element_type=F32)
    q = lax.dot_general(
        y, weights.astype(BF), (((0,), (0,)), ((), ())), preferred_element_type=F32
    ) / (members - 1)
    qs[k_now] = q.astype(BF)

    for k in range(total - 1):

        @pl.when(k_now == k)
        def _(k=k):
            qk = qs[k]
            for b in range(k + 1, total):
                base = 2**b - 1
                for s in range(0, 2**b, 2 ** (k + 1)):
                    keep, move = base + s, base + s + 2**k
                    source = ps[move]
                    change = jnp.dot(source, qk, preferred_element_type=F32)
                    ps[keep] = (
                        ps[keep].astype(F32) + source.astype(F32) - change[:, :members]
                    ).astype(BF)
                    ms[keep] = ms[keep] + ms[move] - change[:, members:]

    @pl.when(k_now == batches - 1)
    def _():
        c_ref[0] = jnp.zeros(c_ref.shape[1:], BF)
        own = pl.ds(pl.multiple_of(own_ref[0] * width, width), width)
        for k in range(total - 1, -1, -1):
            term = jnp.concatenate([qs[k, :, own], qs[k, :, members:]], axis=1)
            c_ref[2**k] = term
            for s in range(2 ** (k + 1), 2**total, 2 ** (k + 1)):
                prior = c_ref[s]
                c_ref[s + 2**k] = (
                    prior.astype(F32)
                    + term.astype(F32)
                    - jnp.dot(qs[k, :, :members], prior, preferred_element_type=F32)
                ).astype(BF)


def final_kernel(history, x_ref, all_ref, mean_ref, c_ref, out_ref, mean_out):
    groups, _, width = all_ref.shape
    change = jnp.zeros((x_ref.shape[1], 2 * width), F32)
    for g in range(groups):
        change += jnp.dot(
            all_ref[g], c_ref[0, g * width : (g + 1) * width, :], preferred_element_type=F32
        )
    out_ref[0] = (x_ref[0].astype(F32) - change[:, :width]).astype(BF)
    shift = change[:, width:].T[0:1, :]
    mean_out[0] = mean_ref[0] - shift


def body(
    anomalies,
    mean_state,
    footprints,
    slot_tiles,
    slot_counts,
    obs_values,
    obs_errors,
    owners,
    batch_order,
):
    batches, _, slot_dev, obs, tile_cells = footprints.shape
    width = anomalies.shape[2]
    groups = lax.axis_size("member")
    members = width * groups
    tiles = anomalies.shape[1] // tile_cells
    mats = 2**batches - 1
    x = anomalies[0].reshape(tiles, tile_cells, width)
    means = mean_state[0].reshape(tiles, 1, tile_cells)
    x_all = lax.all_gather(anomalies[0], "member", axis=0)

    ids = slot_tiles[:, 0][batch_order]
    counts = slot_counts[:, 0, 0][batch_order]
    live = jnp.arange(slot_dev)[None, :] < counts[:, None]
    tile_live = jnp.any(
        (ids[:, :, None] == jnp.arange(tiles)) & live[:, :, None], axis=1
    ).astype(jnp.int32)
    bits = jnp.left_shift(1, jnp.arange(batches))[:, None] * tile_live
    history = jnp.sum(bits, axis=0)
    before = jnp.cumsum(bits, axis=0) - bits
    slot_before = jnp.take_along_axis(before, ids, axis=1)
    base = (jnp.left_shift(1, jnp.arange(batches)) - 1)[:, None]
    dest = jnp.where(live, base + slot_before, mats).astype(jnp.int32).reshape(-1)

    mean_pad = jnp.pad(
        mean_state[0].astype(BF).reshape(tiles, tile_cells, 1), ((0, 0), (0, 0), (0, width - 1))
    )
    x_mean = jnp.concatenate([x, mean_pad], axis=2)
    part, part_mean = pl.pallas_call(
        prints_kernel,
        out_shape=(
            jax.ShapeDtypeStruct((mats, obs, width), BF),
            jax.ShapeDtypeStruct((mats, obs, width), F32),
        ),
        grid_spec=pltpu.PrefetchScalarGridSpec(
            num_scalar_prefetch=3,
            grid=(batches * slot_dev,),
            in_specs=[
                pl.BlockSpec(
                    (1, 1, obs, tile_cells),
                    lambda i, o, t, d: (o[i // slot_dev], i % slot_dev, 0, 0),
                ),
                pl.BlockSpec((1, tile_cells, 2 * width), lambda i, o, t, d: (t[i], 0, 0)),
            ],
            out_specs=[
                pl.BlockSpec((mats, obs, width), lambda i, o, t, d: (0, 0, 0)),
                pl.BlockSpec((mats, obs, width), lambda i, o, t, d: (0, 0, 0)),
            ],
            scratch_shapes=[pltpu.VMEM((mats + 1, obs, 2 * width), F32)],
        ),
        compiler_params=pltpu.CompilerParams(vmem_limit_bytes=40 * 2**20),
        name="prints",
    )(batch_order, ids.reshape(-1), dest, footprints[:, 0], x_mean)

    small = jnp.concatenate(
        [part_mean[:, :, 0], obs_values[0], obs_errors[0]], axis=0
    )
    small_all = lax.all_gather(small, ("space", "lag"), axis=0)
    mean_sum = jnp.sum(small_all[:, :mats], axis=0)
    lags = lax.axis_size("lag")
    owner_row = owners[batch_order] * lags
    values = small_all[owner_row, mats + batch_order]
    errors = small_all[owner_row, mats + batches + batch_order]

    summed = lax.psum_scatter(
        part.reshape(mats * obs, width), ("lag", "space"), scatter_dimension=0, tiled=True
    )
    summed, values, errors, mean_sum = lax.optimization_barrier(
        (summed, values, errors, mean_sum)
    )
    p_half = lax.all_gather(summed, ("member", "space"), axis=0, tiled=True)
    p_all = lax.all_gather(p_half, "lag", axis=0)
    p_all = p_all.reshape(lags, groups, mats, obs // lags, width)
    own = lax.axis_index("member").astype(jnp.int32).reshape(1)
    mean_cols = jnp.pad(mean_sum[:, :, None], ((0, 0), (0, 0), (0, width - 1)))

    states = pl.pallas_call(
        chain_kernel,
        out_shape=jax.ShapeDtypeStruct((2**batches, members, 2 * width), BF),
        grid_spec=pltpu.PrefetchScalarGridSpec(
            num_scalar_prefetch=1,
            grid=(batches,),
            in_specs=[
                pl.BlockSpec(
                    (lags, groups, mats, obs // lags, width), lambda k, o: (0, 0, 0, 0, 0)
                ),
                pl.BlockSpec((mats, obs, width), lambda k, o: (0, 0, 0)),
                pl.BlockSpec((1, obs, 1), lambda k, o: (k, 0, 0)),
                pl.BlockSpec((1, obs, 1), lambda k, o: (k, 0, 0)),
            ],
            out_specs=pl.BlockSpec(
                (2**batches, members, 2 * width), lambda k, o: (0, 0, 0)
            ),
            scratch_shapes=[
                pltpu.VMEM((mats, obs, members), BF),
                pltpu.VMEM((mats, obs, width), F32),
                pltpu.VMEM((batches, members, members + width), BF),
                pltpu.VMEM((obs, obs), F32),
                pltpu.VMEM((obs, obs), F32),
                pltpu.VMEM((obs, obs), F32),
            ],
        ),
        compiler_params=pltpu.CompilerParams(vmem_limit_bytes=56 * 2**20),
        cost_estimate=pl.CostEstimate(
            flops=20 * 10**9, bytes_accessed=10**7, transcendentals=0
        ),
        name="chain",
    )(own, p_all, mean_cols, values[:, :, None], errors[:, :, None])

    new_x, new_mean = pl.pallas_call(
        final_kernel,
        out_shape=(
            jax.ShapeDtypeStruct((tiles, tile_cells, width), BF),
            jax.ShapeDtypeStruct((tiles, 1, tile_cells), F32),
        ),
        grid_spec=pltpu.PrefetchScalarGridSpec(
            num_scalar_prefetch=1,
            grid=(tiles,),
            in_specs=[
                pl.BlockSpec((1, tile_cells, width), lambda t, h: (t, 0, 0)),
                pl.BlockSpec((groups, tile_cells, width), lambda t, h: (0, t, 0)),
                pl.BlockSpec((1, 1, tile_cells), lambda t, h: (t, 0, 0)),
                pl.BlockSpec((1, members, 2 * width), lambda t, h: (h[t], 0, 0)),
            ],
            out_specs=[
                pl.BlockSpec((1, tile_cells, width), lambda t, h: (t, 0, 0)),
                pl.BlockSpec((1, 1, tile_cells), lambda t, h: (t, 0, 0)),
            ],
        ),
        name="final",
    )(history, x, x_all, means, states)
    return (new_x.reshape(1, -1, width), new_mean.reshape(1, -1))


def solution(mesh):
    return jax.shard_map(
        body,
        mesh=mesh,
        in_specs=(
            P("lag", "space", "member"),
            P("lag", "space"),
            P(None, "lag", "space", None, None),
            P(None, "lag", "space"),
            P(None, "lag", "space"),
            P("space", None, None),
            P("space", None, None),
            P(),
            P(),
        ),
        out_specs=(P("lag", "space", "member"), P("lag", "space")),
        check_vma=False,
    )
```
